32 devices in a mesh: sfc: 32 (over z, y, x, core).
Axes of the slice: x: 2, y: 2, z: 4, core: 2. Of those that a mesh axis runs over, the one named last changes fastest.
Arguments:
- rhs: float32 [4, 4, 4, 4096], P(None, None, None, 'sfc'), may hold values from -6 to 6
- screen: float32 [4, 4, 4, 4096], P(None, None, None, 'sfc'), may hold values from 0.05 to 2
- guess: float32 [4, 4, 4, 4096], P(None, None, None, 'sfc'), may hold values from -3 to 3
- counts: int32 [32], replicated, may hold values from 32 to 128, as said below
- neighbours: int32 [6, 4096], P(None, 'sfc'), may hold values from -1 to 263, as said below
Outputs:
- solution: float32 [4, 4, 4, 4096], P(None, None, None, 'sfc')
The draws below stay inside these ranges and needn't reach their ends.
Inputs may be any that keep to these rules, and one draw needn't show every extreme that they name: `counts`: each count is a multiple of 8; one device holds 128 live blocks and another 128 // 4. `neighbours`: A code (d + 1) * 128 + s names slot s of the device d places further along, d in -1, 0, 1, always a live slot; a block on the previous device is among its last 8 live slots and then the naming block is among the first 8 slots, a block on the next device is among its first 8 slots and then the naming block is among the last 8 live slots; dead slots name none.
All inputs are finite; a program needn't handle non-finite values.
Results may differ from the reference program's by a relative error of at most 0.0001.
Values sent between devices are 32-bit elements; how exact they have to be, the bound alone decides.
A program may use at most 64 MiB of HBM per device.

```python
import math
import jax
import jax.numpy as jnp
from jax import lax

SLOTS = 128
EDGE = 4
SWEEPS = 2
BLOCKS = 4096
N_SFC = 32


def live_counts(key):
    base = jax.random.fold_in(key, 71)
    drawn = jax.random.randint(jax.random.fold_in(base, 1), (N_SFC,), SLOTS // 32, SLOTS // 8 + 1) * 8
    fullest = jax.random.randint(jax.random.fold_in(base, 2), (), 0, N_SFC)
    emptiest = (fullest + 1 + jax.random.randint(jax.random.fold_in(base, 3), (), 0, N_SFC - 1)) % N_SFC
    ranks = jnp.arange(N_SFC)
    drawn = jnp.where(ranks == fullest, SLOTS, drawn)
    drawn = jnp.where(ranks == emptiest, SLOTS // 4, drawn)
    return drawn.astype(jnp.int32)


def draw_counts(key, part):
    return live_counts(key)


def draw_neighbours(key, part):
    counts = live_counts(key)
    rim_size = SLOTS // 16
    base = jax.random.fold_in(key, 83)
    index = jnp.arange(N_SFC * SLOTS)
    owner = index // SLOTS
    within = index % SLOTS
    own_live = counts[owner]
    left_live = counts[jnp.maximum(owner - 1, 0)]
    shape = (6, N_SFC * SLOTS)
    boundary = jax.random.randint(jax.random.fold_in(base, 1), shape, 0, 10) == 0
    remote = jax.random.randint(jax.random.fold_in(base, 2), shape, 0, 2) == 1
    leftward = jax.random.randint(jax.random.fold_in(base, 3), shape, 0, 2) == 0
    local_slot = jax.random.randint(jax.random.fold_in(base, 4), shape, 0, 1 << 20) % own_live
    offset = jax.random.randint(jax.random.fold_in(base, 5), shape, 0, rim_size)
    left_ok = (within < rim_size) & (owner > 0)
    right_ok = (within >= own_live - rim_size) & (owner < N_SFC - 1)
    go_left = remote & left_ok & (leftward | jnp.logical_not(right_ok))
    go_right = remote & right_ok & jnp.logical_not(go_left)
    code = jnp.where(go_left, left_live - rim_size + offset, jnp.where(go_right, 2 * SLOTS + offset, SLOTS + local_slot))
    dead = within >= own_live
    code = jnp.where(boundary | dead, -1, code)
    return code.astype(jnp.int32)


def levels(rng, shape, split, least, high):
    level, own = 1.0, jax.random.fold_in(rng, 6)
    for position, blocks in split:
        heights = jnp.exp(jax.random.uniform(jax.random.fold_in(own, position), (blocks,), jnp.float32, least / len(split), high / len(split)))
        level = level * jnp.repeat(heights, shape[position] // blocks).reshape([-1 if axis == position else 1 for axis in range(len(shape))])
    return level


def centred(rng, extent, deviation, limit, shards=(), kind=jnp.bfloat16):
    values = deviation * jax.random.normal(rng, extent, jnp.float32)
    if shards:
        values = values * levels(rng, extent, shards, -0.22, 0.18)
    return jnp.clip(values, -limit, limit).astype(kind)


def setup_inputs(seed: int = 0) -> dict:
    key_list = jax.random.split(jax.random.key(seed), 6)
    return {
        "rhs": centred(key_list[0], (EDGE, EDGE, EDGE, BLOCKS), 1.0, 6.0, ((3, 32),), jnp.float32),
        "screen": jnp.clip(jnp.exp(math.log(2.0) - 3.6888794 * jax.random.uniform(key_list[1], (EDGE, EDGE, EDGE, BLOCKS), jnp.float32) ** levels(key_list[1], (EDGE, EDGE, EDGE, BLOCKS), ((3, 32),), -0.2, 0.2)), 0.05, 2.0),
        "guess": centred(key_list[2], (EDGE, EDGE, EDGE, BLOCKS), 0.5, 3.0, ((3, 32),), jnp.float32),
        "counts": draw_counts(jax.random.fold_in(key_list[5], 71), 0),
        "neighbours": draw_neighbours(jax.random.fold_in(key_list[5], 71), 0),
    }


OMEGA = 0.8
COARSE = 8.0


def lower_pad(values, face, along):
    edge_count = values.shape[along]
    return jnp.concatenate([face, lax.slice_in_dim(values, 0, edge_count - 1, axis=along)], axis=along)


def upper_pad(values, face, along):
    edge_count = values.shape[along]
    return jnp.concatenate([lax.slice_in_dim(values, 1, edge_count, axis=along), face], axis=along)


def neighbour_total(values, source, columns):
    total = jnp.zeros_like(values)
    for along in range(3):
        edge_count = values.shape[along]
        for upward in range(2):
            column = columns[2 * along + upward]
            valid = (column >= 0).astype(jnp.float32)
            safe = jnp.where(column >= 0, column, 0).astype(jnp.int32)
            edge = edge_count - 1 if upward == 0 else 0
            face = lax.slice_in_dim(source, edge, edge + 1, axis=along)
            face = jnp.take(face, safe, axis=3) * valid
            if upward == 0:
                total = total + lower_pad(values, face, along)
            else:
                total = total + upper_pad(values, face, along)
    return total


def relax(values, forcing, screening, columns, live):
    diagonal = 6.0 + screening
    defect = forcing - (diagonal * values - neighbour_total(values, values, columns))
    return jnp.where(live, values + OMEGA * defect / diagonal, 0.0)


def defect_of(values, forcing, screening, columns, live):
    diagonal = 6.0 + screening
    return jnp.where(live, forcing - (diagonal * values - neighbour_total(values, values, columns)), 0.0)


def restrict(values):
    half = values.shape[0] // 2
    width = values.shape[3]
    return values.reshape(half, 2, half, 2, half, 2, width).sum(axis=(1, 3, 5)) * 0.5


def prolong(values):
    return jnp.repeat(jnp.repeat(jnp.repeat(values, 2, axis=0), 2, axis=1), 2, axis=2)


def reference(rhs, screen, guess, counts, neighbours):
    total_slots = rhs.shape[3]
    index = jnp.arange(total_slots, dtype=jnp.int32)
    owner = (index // SLOTS).astype(jnp.int32)
    live = (index % SLOTS) < jnp.take(counts, owner)
    columns = jnp.where(neighbours >= 0, owner * SLOTS + neighbours - SLOTS, -1).astype(jnp.int32)
    forcings = [jnp.where(live, rhs, 0.0)]
    screens = [jnp.where(live, screen, 0.0)]
    current = jnp.where(live, guess, 0.0)
    kept = []
    defect = None
    for depth in range(3):
        for sweep_index in range(SWEEPS):
            current = relax(current, forcings[depth], screens[depth], columns, live)
        kept.append(current)
        defect = defect_of(current, forcings[depth], screens[depth], columns, live)
        if depth < 2:
            forcings.append(restrict(defect))
            screens.append(restrict(screens[depth]))
            current = jnp.zeros_like(forcings[depth + 1])
    grouped = defect.reshape(N_SFC, SLOTS // 8, 8).sum(axis=2) * 0.5
    levels_coarse = N_SFC.bit_length() - 1
    correction = jnp.zeros_like(grouped)
    for section_index in range(levels_coarse + 1):
        group_size = 2 ** section_index
        sums = grouped.reshape(N_SFC // group_size, group_size, SLOTS // 8).sum(axis=1)
        correction = correction + jnp.repeat(sums, group_size, axis=0) / (COARSE * group_size)
    spread = jnp.repeat(correction.reshape(-1), 8).reshape(1, 1, 1, total_slots)
    current = kept[2] + jnp.where(live, spread, 0.0)
    for depth in (2, 1, 0):
        if depth < 2:
            current = kept[depth] + jnp.where(live, prolong(current), 0.0)
        for sweep_index in range(SWEEPS):
            current = relax(current, forcings[depth], screens[depth], columns, live)
    return current
```

```python
import jax
import jax.numpy as jnp
from jax import lax
from jax.experimental import pallas as pl
from jax.experimental.pallas import tpu as pltpu
from jax.sharding import PartitionSpec as P

OMEGA = 0.8
COARSE = 8.0
EXCHANGES = 13
RIM = 8
STAGE_BITS = 5
MESH = pl.DeviceIdType.MESH


def lanes_of(values, index):
    return jnp.take_along_axis(values, index, axis=1, mode="promise_in_bounds")


def rows_of(values, index):
    return jnp.take_along_axis(values, index, axis=0, mode="promise_in_bounds")


def stages_of(devices):
    bits, low, stages = devices.bit_length() - 1, 0, []
    while low < bits:
        take = min(STAGE_BITS, bits - low)
        stages.append((low, take))
        low += take
    return stages


def cycle_kernel(
    devices, slots, counts, rhs, screen, guess, neighbours, out,
    pack, halo, sums, own, halo_send, halo_recv, sum_send, sum_recv,
):
    rank = lax.axis_index("sfc")
    before = lax.rem(rank + devices - 1, devices)
    after = lax.rem(rank + 1, devices)
    stages = stages_of(devices)

    def member(stage, place):
        low, bits = stage
        mine = lax.rem(rank // 2**low, 2**bits)
        return rank + (lax.rem(mine + place, 2**bits) - mine) * 2**low

    barrier = pltpu.get_barrier_semaphore()
    greeted = 0
    for target in (before, after):
        pl.semaphore_signal(barrier, inc=1, device_id=(target,), device_id_type=MESH)
        greeted += 1
    for stage in stages:
        for place in range(1, 2 ** stage[1]):
            pl.semaphore_signal(barrier, inc=1, device_id=(member(stage, place),), device_id_type=MESH)
            greeted += 1

    tile = (8, slots)
    sub = lax.broadcasted_iota(jnp.int32, tile, 0)
    lane = lax.broadcasted_iota(jnp.int32, tile, 1)
    live_own = counts[rank]
    live_before = counts[before]
    live = lane < live_own
    bits = [(sub & (4 >> a)) != 0 for a in range(3)]
    flips = [sub ^ (4 >> a) for a in range(3)]
    half = slots // 2

    pack_index = (lane & (RIM - 1)) + jnp.where(lane < half, live_own - RIM, 0)
    pack_place = (lane & (half - 1)) // RIM

    def decode(code):
        inside = (code >= slots) & (code < 2 * slots)
        outside = (code >= 0) & jnp.logical_not(inside)
        local = jnp.where(inside, code - slots, 0)
        off = jnp.where(code < slots, code - (live_before - RIM), half + code - 2 * slots)
        return inside, outside, local, jnp.where(outside, off & (slots - 1), 0)

    codes = [jnp.broadcast_to(neighbours[k : k + 1, :], tile) for k in range(6)]
    sided = [decode(jnp.where(bits[a], codes[2 * a], codes[2 * a + 1])) for a in range(3)]
    taker = [decode(jnp.where(bits[a], codes[2 * a + 1], codes[2 * a])) for a in range(3)]
    every = jnp.full(tile, -1, jnp.int32)
    for k in range(6):
        every = jnp.where(sub == k, codes[k], every)
    every = decode(every)

    first, second = (sub & 1) + ((sub >> 1) & 1) * 4, (sub & 1) + ((sub >> 1) & 1) * 4 + 2

    def load(ref):
        rows = [ref[8 * t : 8 * t + 8, :] for t in range(8)]
        result = []
        for hx in range(2):
            for hy in range(2):
                low, high = rows[4 * hx + hy], rows[4 * hx + 2 + hy]
                for index in (first, second):
                    result.append(jnp.where(sub < 4, rows_of(low, index), rows_of(high, index)))
        return result

    copies = []
    state = {"step": 0, "ready": False}

    def begin(packed):
        step = state["step"]
        state["step"] = step + 1
        pack[step] = packed
        if not state["ready"]:
            pl.semaphore_wait(barrier, greeted)
            state["ready"] = True
        pair = []
        for side, target in ((0, after), (1, before)):
            copy = pltpu.make_async_remote_copy(
                src_ref=pack.at[step],
                dst_ref=halo.at[step, side],
                send_sem=halo_send.at[step, side],
                recv_sem=halo_recv.at[step, side],
                device_id=(target,),
                device_id_type=MESH,
            )
            copy.start()
            pair.append(copy)
        copies.extend(pair)
        return step, pair

    def finish(handle):
        step, pair = handle
        for copy in pair:
            copy.wait_recv()
        return jnp.where(lane < half, halo[step, 0], halo[step, 1])

    def total_fine(values):
        packed = jnp.zeros(tile, jnp.float32)
        for j in range(8):
            packed = jnp.where(pack_place == j, lanes_of(values[j], pack_index), packed)
        handle = begin(packed)
        sums_here = [None] * 8
        for a in range(3):
            stride = 4 >> a
            inside, _, local, _ = sided[a]
            for j in range(8):
                if j & stride:
                    continue
                low, high = values[j], values[j + stride]
                across = jnp.where(inside, lanes_of(jnp.where(bits[a], high, low), local), 0.0)
                for place, part in (
                    (j, low + jnp.where(bits[a], across, high)),
                    (j + stride, high + jnp.where(bits[a], low, across)),
                ):
                    part = rows_of(part, flips[a])
                    sums_here[place] = part if sums_here[place] is None else sums_here[place] + part
        received = finish(handle)
        for a in range(3):
            stride = 4 >> a
            _, outside, _, off = taker[a]
            turned = rows_of(received, flips[a])
            base = off + jnp.where(bits[a], 0, RIM * stride)
            for j in range(8):
                if j & stride:
                    continue
                got = jnp.where(outside, lanes_of(turned, (base + RIM * j) & (slots - 1)), 0.0)
                sums_here[j] = sums_here[j] + jnp.where(bits[a], 0.0, got)
                sums_here[j + stride] = sums_here[j + stride] + jnp.where(bits[a], got, 0.0)
        return sums_here

    def total_middle(values):
        values = values[0]
        handle = begin(lanes_of(values, pack_index))
        total = jnp.zeros(tile, jnp.float32)
        for a in range(3):
            inside, _, local, _ = sided[a]
            total = total + rows_of(values + jnp.where(inside, lanes_of(values, local), 0.0), flips[a])
        received = finish(handle)
        for a in range(3):
            _, outside, _, off = taker[a]
            total = total + jnp.where(outside, lanes_of(rows_of(received, flips[a]), off), 0.0)
        return [total]

    def total_coarse(values):
        values = values[0]
        handle = begin(lanes_of(values, pack_index))
        inside, outside, local, off = every
        part = jnp.where(inside, lanes_of(values, local), 0.0)
        part = part + jnp.where(outside, lanes_of(finish(handle), off), 0.0)
        return [jnp.broadcast_to(part.sum(axis=0, keepdims=True), tile)]

    totals = (total_fine, total_middle, total_coarse)

    def masked(values):
        return [jnp.where(live, v, 0.0) for v in values]

    def sweep(depth, values, forcing, weight):
        found = totals[depth](values)
        return [(1.0 - OMEGA) * v + w * (f + t) for v, f, w, t in zip(values, forcing, weight, found)]

    def defect_of(depth, values, forcing, diagonal):
        found = totals[depth](values)
        return [jnp.where(live, f - (d * v - t), 0.0) for v, f, d, t in zip(values, forcing, diagonal, found)]

    def stacked(rows):
        result = jnp.broadcast_to(rows[0], tile)
        for j in range(1, 8):
            result = jnp.where(sub == j, rows[j], result)
        return result

    def restrict(depth, values):
        if depth == 0:
            return [stacked([v.sum(axis=0, keepdims=True) * 0.5 for v in values])]
        return [jnp.broadcast_to(values[0].sum(axis=0, keepdims=True) * 0.5, tile)]

    def prolong(depth, values):
        if depth == 0:
            return [jnp.broadcast_to(values[0][j : j + 1, :], tile) for j in range(8)]
        return values

    forcing = masked(load(rhs))
    screening = masked(load(screen))
    current = masked(load(guess))
    levels = []
    for depth in range(3):
        diagonal = [6.0 + s for s in screening]
        weight = masked([OMEGA / d for d in diagonal])
        if depth == 0:
            current = sweep(depth, current, forcing, weight)
        else:
            current = [w * f for w, f in zip(weight, forcing)]
        current = sweep(depth, current, forcing, weight)
        levels.append((current, forcing, weight))
        defect = defect_of(depth, current, forcing, diagonal)
        if depth < 2:
            forcing, screening = restrict(depth, defect), restrict(depth, screening)

    grouped = defect[0]
    for distance in (1, 2, 4):
        grouped = grouped + lanes_of(grouped, lane ^ distance)
    running = grouped[0:1, :] * 0.5
    correction = running / COARSE
    start = 0
    for number, stage in enumerate(stages):
        low, count = stage
        size = 2**count
        own[number] = running
        group = []
        for place in range(1, size):
            copy = pltpu.make_async_remote_copy(
                src_ref=own.at[number],
                dst_ref=sums.at[start + place],
                send_sem=sum_send.at[start + place],
                recv_sem=sum_recv.at[start + place],
                device_id=(member(stage, place),),
                device_id_type=MESH,
            )
            copy.start()
            group.append(copy)
        copies.extend(group)
        mine = lax.rem(rank // 2**low, size)
        own_weight = sum(1.0 / (COARSE * 2 ** (low + k)) for k in range(1, count + 1))
        correction = correction + own_weight * running
        for place, copy in enumerate(group, 1):
            copy.wait_recv()
            sender = lax.rem(mine - place + size, size)
            factor = jnp.float32(0.0)
            for k in range(1, count + 1):
                same = (mine // 2**k) == (sender // 2**k)
                factor = factor + jnp.where(same, 1.0 / (COARSE * 2 ** (low + k)), 0.0)
            arrived = sums[start + place]
            correction = correction + factor * arrived
            running = running + arrived
        start += size

    current = [jnp.broadcast_to(correction, tile)]
    for depth in (2, 1, 0):
        kept, forcing, weight = levels[depth]
        raised = current if depth == 2 else prolong(depth, current)
        current = [a + b for a, b in zip(kept, masked(raised))]
        for _ in range(2):
            current = sweep(depth, current, forcing, weight)

    spread = (sub & 1) + (sub >> 2) * 2
    upper = (sub & 2) != 0
    for hx in range(2):
        for hy in range(2):
            near, far = current[4 * hx + 2 * hy], current[4 * hx + 2 * hy + 1]
            for bx in range(2):
                row = 8 * (4 * hx + 2 * bx + hy)
                index = spread + 4 * bx
                out[row : row + 8, :] = jnp.where(upper, rows_of(far, index), rows_of(near, index))
    for copy in copies:
        copy.wait_send()


def per_device(rhs, screen, guess, counts, neighbours):
    shape = rhs.shape
    slots = shape[3]
    devices = lax.axis_size("sfc")
    stages = stages_of(devices)
    places = max(1, sum(2**count for _, count in stages))
    rows = shape[0] * shape[1] * shape[2]
    vmem = pl.BlockSpec(memory_space=pltpu.VMEM)
    result = pl.pallas_call(
        lambda *refs: cycle_kernel(devices, slots, *refs),
        out_shape=jax.ShapeDtypeStruct((rows, slots), jnp.float32),
        in_specs=[pl.BlockSpec(memory_space=pltpu.SMEM)] + [vmem] * 4,
        out_specs=vmem,
        scratch_shapes=[
            pltpu.VMEM((EXCHANGES, 8, slots), jnp.float32),
            pltpu.VMEM((EXCHANGES, 2, 8, slots), jnp.float32),
            pltpu.VMEM((places, 1, slots), jnp.float32),
            pltpu.VMEM((max(1, len(stages)), 1, slots), jnp.float32),
            pltpu.SemaphoreType.DMA((EXCHANGES, 2)),
            pltpu.SemaphoreType.DMA((EXCHANGES, 2)),
            pltpu.SemaphoreType.DMA((places,)),
            pltpu.SemaphoreType.DMA((places,)),
        ],
        compiler_params=pltpu.CompilerParams(collective_id=0, has_side_effects=True),
        name="cycle",
    )(counts, rhs.reshape(rows, slots), screen.reshape(rows, slots), guess.reshape(rows, slots), neighbours)
    return result.reshape(shape)


def solution(mesh):
    blocks = P(None, None, None, "sfc")
    return jax.shard_map(
        per_device,
        mesh=mesh,
        in_specs=(blocks, blocks, blocks, P(), P(None, "sfc")),
        out_specs=blocks,
        check_vma=False,
    )
```

```python
import jax
import jax.numpy as jnp
from jax import lax
from jax.experimental import pallas as pl
from jax.experimental.pallas import tpu as pltpu
from jax.sharding import PartitionSpec as P

OMEGA = 0.8
COARSE = 8.0
RIM = 8
REACH = 3
MESH = pl.DeviceIdType.MESH


def lanes_of(values, index):
    return jnp.take_along_axis(values, index, axis=1, mode="promise_in_bounds")


def rows_of(values, index):
    return jnp.take_along_axis(values, index, axis=0, mode="promise_in_bounds")


def cycle_kernel(
    devices, slots, counts, rhs, screen, guess, neighbours, out,
    near, rim, codes, middle, fine, coarse, sums, tree,
    rim_out, middle_out, fine_out, coarse_out, send_sem, recv_sem,
):
    rank = lax.axis_index("sfc")

    def at(offset):
        return lax.rem(rank + offset + devices, devices)

    barrier = pltpu.get_barrier_semaphore()
    for offset in range(1, devices):
        pl.semaphore_signal(barrier, inc=1, device_id=(at(offset),), device_id_type=MESH)

    tile = (8, slots)
    sub = lax.broadcasted_iota(jnp.int32, tile, 0)
    lane = lax.broadcasted_iota(jnp.int32, tile, 1)
    bits = [(sub & (4 >> a)) != 0 for a in range(3)]
    flips = [sub ^ (4 >> a) for a in range(3)]
    half = slots // 2
    live_of = {j: counts[at(j)] for j in range(-REACH - 1, REACH + 1)}
    live = {j: lane < live_of[j] for j in range(-REACH, REACH + 1)}

    pack_place = (lane & (half - 1)) // RIM
    pack_index = {
        j: (lane & (RIM - 1)) + jnp.where(lane < half, live_of[j] - RIM, 0)
        for j in range(-REACH, REACH + 1)
    }

    copies = []

    def send(source, target, offset):
        number = len(copies)
        copy = pltpu.make_async_remote_copy(
            src_ref=source,
            dst_ref=target,
            send_sem=send_sem.at[number],
            recv_sem=recv_sem.at[number],
            device_id=(at(offset),),
            device_id_type=MESH,
        )
        copy.start()
        copies.append(copy)
        return copy

    def place(offset, reach):
        return offset + reach if offset < 0 else offset + reach - 1

    def offsets(reach):
        return [sign * step for step in range(1, reach + 1) for sign in (1, -1)]

    first = (sub & 1) + ((sub >> 1) & 1) * 4

    def load(ref, *lead):
        rows = [ref[(*lead, slice(8 * t, 8 * t + 8), slice(None))] for t in range(8)]
        result = []
        for hx in range(2):
            for hy in range(2):
                low, high = rows[4 * hx + hy], rows[4 * hx + 2 + hy]
                for index in (first, first + 2):
                    result.append(jnp.where(sub < 4, rows_of(low, index), rows_of(high, index)))
        return result

    def masked(part, values):
        return [jnp.where(live[part], v, 0.0) for v in values]

    def packed(part, values):
        if len(values) == 1:
            return lanes_of(values[0], pack_index[part])
        result = lanes_of(values[0], pack_index[part])
        for j in range(1, 8):
            result = jnp.where(pack_place == j, lanes_of(values[j], pack_index[part]), result)
        return result

    forcing, screening, current = ({0: masked(0, load(r))} for r in (rhs, screen, guess))
    rim_out[...] = packed(0, current[0])
    pl.semaphore_wait(barrier, devices - 1)
    arrive = {}
    for o in offsets(2)[2:]:
        arrive["rim", -o] = send(rim_out, rim.at[place(-o, 2) // 3], o)
    for o in offsets(1):
        for k, ref in enumerate((guess, rhs, screen)):
            arrive["near", -o, k] = send(ref, near.at[place(-o, 1), k], o)
    for o in offsets(REACH):
        arrive["codes", -o] = send(neighbours, codes.at[place(-o, REACH)], o)

    def decoded(part, code):
        inside = (code >= slots) & (code < 2 * slots)
        outside = (code >= 0) & jnp.logical_not(inside)
        local = jnp.where(inside, code - slots, 0)
        off = jnp.where(code < slots, code - (live_of[part - 1] - RIM), half + code - 2 * slots)
        return inside, outside, local, jnp.where(outside, off & (slots - 1), 0)

    tables = {}

    def table(part):
        if part not in tables:
            if part:
                arrive["codes", part].wait_recv()
                ref = codes.at[place(part, REACH)]
            else:
                ref = neighbours
            rows = [jnp.broadcast_to(ref[k : k + 1, :], tile) for k in range(6)]
            sided = [decoded(part, jnp.where(bits[a], rows[2 * a], rows[2 * a + 1])) for a in range(3)]
            taker = [decoded(part, jnp.where(bits[a], rows[2 * a + 1], rows[2 * a])) for a in range(3)]
            every = jnp.full(tile, -1, jnp.int32)
            for k in range(6):
                every = jnp.where(sub == k, rows[k], every)
            tables[part] = (sided, taker, decoded(part, every))
        return tables[part]

    def total_fine(part, values, received):
        sided, taker, _ = table(part)
        total = [None] * 8
        for a in range(3):
            stride = 4 >> a
            inside, _, local, _ = sided[a]
            _, outside, _, off = taker[a]
            turned = rows_of(received, flips[a])
            base = off + jnp.where(bits[a], 0, RIM * stride)
            for j in range(8):
                if j & stride:
                    continue
                low, high = values[j], values[j + stride]
                across = jnp.where(inside, lanes_of(jnp.where(bits[a], high, low), local), 0.0)
                got = jnp.where(outside, lanes_of(turned, (base + RIM * j) & (slots - 1)), 0.0)
                for where, kept, far in (
                    (j, low + jnp.where(bits[a], across, high), jnp.where(bits[a], 0.0, got)),
                    (j + stride, high + jnp.where(bits[a], low, across), jnp.where(bits[a], got, 0.0)),
                ):
                    piece = rows_of(kept, flips[a]) + far
                    total[where] = piece if total[where] is None else total[where] + piece
        return total

    def total_middle(part, values, received):
        sided, taker, _ = table(part)
        total = None
        for a in range(3):
            inside, _, local, _ = sided[a]
            _, outside, _, off = taker[a]
            piece = rows_of(values[0] + jnp.where(inside, lanes_of(values[0], local), 0.0), flips[a])
            piece = piece + jnp.where(outside, lanes_of(rows_of(received, flips[a]), off), 0.0)
            total = piece if total is None else total + piece
        return [total]

    def total_coarse(part, values, received):
        inside, outside, local, off = table(part)[2]
        piece = jnp.where(inside, lanes_of(values[0], local), 0.0)
        piece = piece + jnp.where(outside, lanes_of(received, off), 0.0)
        return [jnp.broadcast_to(piece.sum(axis=0, keepdims=True), tile)]

    totals = (total_fine, total_middle, total_coarse)

    def total(depth, values, reach, rims=None):
        rims = dict(rims or {})
        for j in values:
            if abs(j) <= reach + 1:
                rims[j] = packed(j, values[j])
        result = {}
        for j in range(-reach, reach + 1):
            lower, upper = rims.get(j - 1), rims.get(j + 1)
            received = upper if lower is None else lower if upper is None else jnp.where(lane < half, lower, upper)
            result[j] = totals[depth](j, values[j], received)
        return result

    def sweep(depth, values, forcing, weight, reach, rims=None):
        found = total(depth, values, reach, rims)
        return {
            j: [(1.0 - OMEGA) * v + w * (f + t) for v, f, w, t in zip(values[j], forcing[j], weight[j], found[j])]
            for j in found
        }

    def defect_of(depth, values, forcing, screening, reach):
        found = total(depth, values, reach)
        return {
            j: masked(j, [f - ((6.0 + s) * v - t) for v, f, s, t in zip(values[j], forcing[j], screening[j], found[j])])
            for j in found
        }

    def weights(screening):
        return {j: masked(j, [OMEGA / (6.0 + s) for s in values]) for j, values in screening.items()}

    def start(forcing, weight):
        return {j: [w * f for w, f in zip(weight[j], forcing[j])] for j in forcing}

    def restrict_fine(values):
        result = jnp.broadcast_to(values[0].sum(axis=0, keepdims=True), tile)
        for j in range(1, 8):
            result = jnp.where(sub == j, values[j].sum(axis=0, keepdims=True), result)
        return [result * 0.5]

    def restrict_middle(values):
        return [jnp.broadcast_to(values[0].sum(axis=0, keepdims=True) * 0.5, tile)]

    for j in (-1, 1):
        for k, field in enumerate((current, forcing, screening)):
            arrive["near", j, k].wait_recv()
            field[j] = masked(j, load(near, place(j, 1), k))
    weight0, forcing0 = weights(screening), forcing
    rims = {}
    for j in (-2, 2):
        arrive["rim", j].wait_recv()
        rims[j] = rim[place(j, 2) // 3]
    current = sweep(0, current, forcing, weight0, 1, rims)
    kept0 = sweep(0, current, forcing, weight0, 1)
    for j in range(8):
        fine_out[j] = kept0[0][j]
    for o in offsets(1):
        arrive["fine", -o] = send(fine_out, fine.at[place(-o, 1)], o)
    defect = defect_of(0, kept0, forcing, screening, 0)
    kept0 = {0: kept0[0]}
    forcing1, screening1 = {0: restrict_fine(defect[0])}, {0: restrict_fine(screening[0])}

    middle_out[0] = forcing1[0][0]
    middle_out[1] = screening1[0][0]
    for o in offsets(REACH):
        arrive["middle", -o] = send(middle_out, middle.at[place(-o, REACH)], o)
    for j in offsets(REACH):
        table(j)
        arrive["middle", j].wait_recv()
        forcing1[j] = [middle[place(j, REACH), 0]]
        screening1[j] = [middle[place(j, REACH), 1]]
    weight1 = weights(screening1)
    kept1 = sweep(1, start(forcing1, weight1), forcing1, weight1, 2)
    forcing2 = {j: restrict_middle(v) for j, v in defect_of(1, kept1, forcing1, screening1, 1).items()}
    screening2 = {j: restrict_middle(v) for j, v in screening1.items()}
    weight2 = weights(screening2)
    kept2 = sweep(2, start(forcing2, weight2), forcing2, weight2, 1)
    grouped = defect_of(2, kept2, forcing2, screening2, 0)[0][0]
    for distance in (1, 2, 4):
        grouped = grouped + lanes_of(grouped, lane ^ distance)

    sums[rank] = grouped[0:1, :] * 0.5
    for k, value in enumerate((kept1, kept2, forcing2)):
        coarse_out[k] = value[0][0]
    arrived = [send(sums.at[rank], sums.at[rank], o) for o in range(1, devices)]
    for o in offsets(REACH):
        arrive["coarse", -o] = send(coarse_out, coarse.at[place(-o, REACH)], o)
    kept1, kept2, forcing2 = {0: kept1[0]}, {0: kept2[0]}, {0: forcing2[0]}
    for copy in arrived:
        copy.wait_recv()
    width, base, bases = devices, 0, []
    row = [sums[d] for d in range(devices)]
    while width > 1:
        width //= 2
        row = [row[2 * i] + row[2 * i + 1] for i in range(width)]
        bases.append(base)
        for i in range(width):
            tree[base + i] = row[i]
        base += width

    current = {}
    for j in [0] + offsets(REACH):
        if j:
            arrive["coarse", j].wait_recv()
            for k, field in enumerate((kept1, kept2, forcing2)):
                field[j] = [coarse[place(j, REACH), k]]
        other = at(j)
        correction = sums[other] / COARSE
        for k, base in enumerate(bases, 1):
            correction = correction + tree[base + other // 2**k] / (COARSE * 2**k)
        current[j] = [kept2[j][0] + jnp.where(live[j], jnp.broadcast_to(correction, tile), 0.0)]
    current = sweep(2, current, forcing2, weight2, 3)
    current = sweep(2, current, forcing2, weight2, 2)
    current = {j: [kept1[j][0] + masked(j, v)[0]] for j, v in current.items()}
    current = sweep(1, current, forcing1, weight1, 2)
    current = sweep(1, current, forcing1, weight1, 1)
    for j in (-1, 1):
        arrive["fine", j].wait_recv()
        kept0[j] = [fine[place(j, 1), k] for k in range(8)]
    current = {
        j: [a + jnp.where(live[j], jnp.broadcast_to(v[0][k : k + 1, :], tile), 0.0) for k, a in enumerate(kept0[j])]
        for j, v in current.items()
    }
    current = sweep(0, current, forcing0, weight0, 1)
    current = sweep(0, current, forcing0, weight0, 0)[0]

    spread = (sub & 1) + (sub >> 2) * 2
    upper = (sub & 2) != 0
    for hx in range(2):
        for hy in range(2):
            low, high = current[4 * hx + 2 * hy], current[4 * hx + 2 * hy + 1]
            for bx in range(2):
                row = 8 * (4 * hx + 2 * bx + hy)
                index = spread + 4 * bx
                out[row : row + 8, :] = jnp.where(upper, rows_of(high, index), rows_of(low, index))
    for copy in copies:
        copy.wait_send()


def per_device(rhs, screen, guess, counts, neighbours):
    shape = rhs.shape
    slots = shape[3]
    devices = lax.axis_size("sfc")
    rows = shape[0] * shape[1] * shape[2]
    vmem = pl.BlockSpec(memory_space=pltpu.VMEM)
    result = pl.pallas_call(
        lambda *refs: cycle_kernel(devices, slots, *refs),
        out_shape=jax.ShapeDtypeStruct((rows, slots), jnp.float32),
        in_specs=[pl.BlockSpec(memory_space=pltpu.SMEM)] + [vmem] * 4,
        out_specs=vmem,
        scratch_shapes=[
            pltpu.VMEM((2, 3, rows, slots), jnp.float32),
            pltpu.VMEM((2, 8, slots), jnp.float32),
            pltpu.VMEM((2 * REACH, *neighbours.shape), jnp.int32),
            pltpu.VMEM((2 * REACH, 2, 8, slots), jnp.float32),
            pltpu.VMEM((2, 8, 8, slots), jnp.float32),
            pltpu.VMEM((2 * REACH, 3, 8, slots), jnp.float32),
            pltpu.VMEM((devices, 1, slots), jnp.float32),
            pltpu.VMEM((devices, 1, slots), jnp.float32),
            pltpu.VMEM((8, slots), jnp.float32),
            pltpu.VMEM((2, 8, slots), jnp.float32),
            pltpu.VMEM((8, 8, slots), jnp.float32),
            pltpu.VMEM((3, 8, slots), jnp.float32),
            pltpu.SemaphoreType.DMA((10 + 6 * REACH + devices - 1,)),
            pltpu.SemaphoreType.DMA((10 + 6 * REACH + devices - 1,)),
        ],
        compiler_params=pltpu.CompilerParams(collective_id=0, has_side_effects=True),
        name="cycle",
    )(counts, rhs.reshape(rows, slots), screen.reshape(rows, slots), guess.reshape(rows, slots), neighbours)
    return result.reshape(shape)


def solution(mesh):
    blocks = P(None, None, None, "sfc")
    return jax.shard_map(
        per_device,
        mesh=mesh,
        in_specs=(blocks, blocks, blocks, P(), P(None, "sfc")),
        out_specs=blocks,
        check_vma=False,
    )
```

```python
import jax
import jax.numpy as jnp
from jax import lax
from jax.experimental import pallas as pl
from jax.experimental.pallas import tpu as pltpu
from jax.sharding import PartitionSpec as P

OMEGA = 0.8
COARSE = 8.0
RIM = 8
REACH = 3
MESH = pl.DeviceIdType.MESH


def lanes_of(values, index):
    return jnp.take_along_axis(values, index, axis=1, mode="promise_in_bounds")


def rows_of(values, index):
    return jnp.take_along_axis(values, index, axis=0, mode="promise_in_bounds")


def cycle_kernel(
    devices, slots, counts, rhs_in, screen_in, guess_in, neighbours_in, out,
    near, rim, codes, middle, fine, coarse, sums, tree,
    rim_out, middle_out, fine_out, coarse_out, own, neighbours, send_sem, recv_sem, load_sem,
):
    rank = lax.axis_index("sfc")

    def at(offset):
        return lax.rem(rank + offset + devices, devices)

    guess, rhs, screen = own.at[0], own.at[1], own.at[2]
    pairs = ((guess_in, guess), (rhs_in, rhs), (screen_in, screen), (neighbours_in, neighbours))
    loads = [pltpu.make_async_copy(a, b, load_sem.at[k]) for k, (a, b) in enumerate(pairs)]
    for copy in loads:
        copy.start()

    barrier = pltpu.get_barrier_semaphore()
    for offset in range(1, devices):
        pl.semaphore_signal(barrier, inc=1, device_id=(at(offset),), device_id_type=MESH)

    tile = (8, slots)
    sub = lax.broadcasted_iota(jnp.int32, tile, 0)
    lane = lax.broadcasted_iota(jnp.int32, tile, 1)
    bits = [(sub & (4 >> a)) != 0 for a in range(3)]
    flips = [sub ^ (4 >> a) for a in range(3)]
    half = slots // 2
    live_of = {j: counts[at(j)] for j in range(-REACH - 1, REACH + 1)}
    live = {j: lane < live_of[j] for j in range(-REACH, REACH + 1)}

    pack_place = (lane & (half - 1)) // RIM
    pack_index = {
        j: (lane & (RIM - 1)) + jnp.where(lane < half, live_of[j] - RIM, 0)
        for j in range(-REACH, REACH + 1)
    }

    copies = []

    def reaches(offset):
        return rank < devices - offset if offset > 0 else rank >= -offset

    class Arrival:
        def __init__(self, copy, offset):
            self.copy, self.offset = copy, offset

        def wait_recv(self):
            if self.offset:
                pl.when(reaches(-self.offset))(self.copy.wait_recv)
            else:
                self.copy.wait_recv()

    def send(source, target, offset, wrap=False):
        number = len(copies)
        copy = pltpu.make_async_remote_copy(
            src_ref=source,
            dst_ref=target,
            send_sem=send_sem.at[number],
            recv_sem=recv_sem.at[number],
            device_id=(at(offset),),
            device_id_type=MESH,
        )
        if wrap:
            copy.start()
        else:
            pl.when(reaches(offset))(copy.start)
        copies.append((copy, 0 if wrap else offset))
        return Arrival(copy, 0 if wrap else offset)

    def place(offset, reach):
        return offset + reach if offset < 0 else offset + reach - 1

    def offsets(reach):
        return [sign * step for step in range(1, reach + 1) for sign in (1, -1)]

    first = (sub & 1) + ((sub >> 1) & 1) * 4

    def load(ref, *lead):
        rows = [ref[(*lead, slice(8 * t, 8 * t + 8), slice(None))] for t in range(8)]
        result = []
        for hx in range(2):
            for hy in range(2):
                low, high = rows[4 * hx + hy], rows[4 * hx + 2 + hy]
                for index in (first, first + 2):
                    result.append(jnp.where(sub < 4, rows_of(low, index), rows_of(high, index)))
        return result

    def masked(part, values):
        return [jnp.where(live[part], v, 0.0) for v in values]

    def packed(part, values):
        if len(values) == 1:
            return lanes_of(values[0], pack_index[part])
        result = lanes_of(values[0], pack_index[part])
        for j in range(1, 8):
            result = jnp.where(pack_place == j, lanes_of(values[j], pack_index[part]), result)
        return result

    for copy in loads:
        copy.wait()
    pl.semaphore_wait(barrier, devices - 1)
    arrive = {}
    for o in offsets(1):
        for k, ref in enumerate((guess, rhs, screen)):
            arrive["near", -o, k] = send(ref, near.at[place(-o, 1), k], o)
        arrive["codes", -o] = send(neighbours, codes.at[place(-o, REACH)], o)
    forcing, screening, current = ({0: masked(0, load(r))} for r in (rhs, screen, guess))
    rim_out[...] = packed(0, current[0])
    for o in offsets(2)[2:]:
        arrive["rim", -o] = send(rim_out, rim.at[place(-o, 2) // 3], o)
    for o in offsets(REACH)[2:]:
        arrive["codes", -o] = send(neighbours, codes.at[place(-o, REACH)], o)

    def decoded(part, code):
        inside = (code >= slots) & (code < 2 * slots)
        outside = (code >= 0) & jnp.logical_not(inside)
        local = jnp.where(inside, code - slots, 0)
        off = jnp.where(code < slots, code - (live_of[part - 1] - RIM), half + code - 2 * slots)
        return inside, outside, local, jnp.where(outside, off & (slots - 1), 0)

    tables = {}

    def table(part):
        if part not in tables:
            if part:
                arrive["codes", part].wait_recv()
                ref = codes.at[place(part, REACH)]
            else:
                ref = neighbours
            rows = [jnp.broadcast_to(ref[k : k + 1, :], tile) for k in range(6)]
            sided = [decoded(part, jnp.where(bits[a], rows[2 * a], rows[2 * a + 1])) for a in range(3)]
            taker = [decoded(part, jnp.where(bits[a], rows[2 * a + 1], rows[2 * a])) for a in range(3)]
            every = jnp.full(tile, -1, jnp.int32)
            for k in range(6):
                every = jnp.where(sub == k, rows[k], every)
            tables[part] = (sided, taker, decoded(part, every))
        return tables[part]

    def total_fine(part, values, received):
        sided, taker, _ = table(part)
        total = [None] * 8
        for a in range(3):
            stride = 4 >> a
            inside, _, local, _ = sided[a]
            _, outside, _, off = taker[a]
            turned = rows_of(received, flips[a])
            base = off + jnp.where(bits[a], 0, RIM * stride)
            for j in range(8):
                if j & stride:
                    continue
                low, high = values[j], values[j + stride]
                across = jnp.where(inside, lanes_of(jnp.where(bits[a], high, low), local), 0.0)
                got = jnp.where(outside, lanes_of(turned, (base + RIM * j) & (slots - 1)), 0.0)
                for where, kept, far in (
                    (j, low + jnp.where(bits[a], across, high), jnp.where(bits[a], 0.0, got)),
                    (j + stride, high + jnp.where(bits[a], low, across), jnp.where(bits[a], got, 0.0)),
                ):
                    piece = rows_of(kept, flips[a]) + far
                    total[where] = piece if total[where] is None else total[where] + piece
        return total

    def total_middle(part, values, received):
        sided, taker, _ = table(part)
        total = None
        for a in range(3):
            inside, _, local, _ = sided[a]
            _, outside, _, off = taker[a]
            piece = rows_of(values[0] + jnp.where(inside, lanes_of(values[0], local), 0.0), flips[a])
            piece = piece + jnp.where(outside, lanes_of(rows_of(received, flips[a]), off), 0.0)
            total = piece if total is None else total + piece
        return [total]

    def total_coarse(part, values, received):
        inside, outside, local, off = table(part)[2]
        piece = jnp.where(inside, lanes_of(values[0], local), 0.0)
        piece = piece + jnp.where(outside, lanes_of(received, off), 0.0)
        return [jnp.broadcast_to(piece.sum(axis=0, keepdims=True), tile)]

    totals = (total_fine, total_middle, total_coarse)

    def total(depth, values, reach, rims=None):
        rims = dict(rims or {})
        for j in values:
            if abs(j) <= reach + 1:
                rims[j] = packed(j, values[j])
        result = {}
        for j in range(-reach, reach + 1):
            lower, upper = rims.get(j - 1), rims.get(j + 1)
            received = upper if lower is None else lower if upper is None else jnp.where(lane < half, lower, upper)
            result[j] = totals[depth](j, values[j], received)
        return result

    def sweep(depth, values, forcing, weight, reach, rims=None):
        found = total(depth, values, reach, rims)
        return {
            j: [(1.0 - OMEGA) * v + w * (f + t) for v, f, w, t in zip(values[j], forcing[j], weight[j], found[j])]
            for j in found
        }

    def defect_of(depth, values, forcing, screening, reach):
        found = total(depth, values, reach)
        return {
            j: masked(j, [f - ((6.0 + s) * v - t) for v, f, s, t in zip(values[j], forcing[j], screening[j], found[j])])
            for j in found
        }

    def weights(screening):
        return {j: masked(j, [OMEGA / (6.0 + s) for s in values]) for j, values in screening.items()}

    def start(forcing, weight):
        return {j: [w * f for w, f in zip(weight[j], forcing[j])] for j in forcing}

    def restrict_fine(values):
        result = jnp.broadcast_to(values[0].sum(axis=0, keepdims=True), tile)
        for j in range(1, 8):
            result = jnp.where(sub == j, values[j].sum(axis=0, keepdims=True), result)
        return [result * 0.5]

    def restrict_middle(values):
        return [jnp.broadcast_to(values[0].sum(axis=0, keepdims=True) * 0.5, tile)]

    for j in (-1, 1):
        for k, field in enumerate((current, forcing, screening)):
            arrive["near", j, k].wait_recv()
            field[j] = masked(j, load(near, place(j, 1), k))
    weight0, forcing0 = weights(screening), forcing
    rims = {}
    for j in (-2, 2):
        arrive["rim", j].wait_recv()
        rims[j] = rim[place(j, 2) // 3]
    current = sweep(0, current, forcing, weight0, 1, rims)
    kept0 = sweep(0, current, forcing, weight0, 1)
    for j in range(8):
        fine_out[j] = kept0[0][j]
    for o in offsets(1):
        arrive["fine", -o] = send(fine_out, fine.at[place(-o, 1)], o)
    defect = defect_of(0, kept0, forcing, screening, 0)
    kept0 = {0: kept0[0]}
    forcing1, screening1 = {0: restrict_fine(defect[0])}, {0: restrict_fine(screening[0])}

    middle_out[0] = forcing1[0][0]
    middle_out[1] = screening1[0][0]
    for o in offsets(REACH):
        arrive["middle", -o] = send(middle_out, middle.at[place(-o, REACH)], o)
    for j in offsets(REACH):
        table(j)
        arrive["middle", j].wait_recv()
        forcing1[j] = [middle[place(j, REACH), 0]]
        screening1[j] = [middle[place(j, REACH), 1]]
    weight1 = weights(screening1)
    kept1 = sweep(1, start(forcing1, weight1), forcing1, weight1, 2)
    forcing2 = {j: restrict_middle(v) for j, v in defect_of(1, kept1, forcing1, screening1, 1).items()}
    screening2 = {j: restrict_middle(v) for j, v in screening1.items()}
    weight2 = weights(screening2)
    kept2 = sweep(2, start(forcing2, weight2), forcing2, weight2, 1)
    grouped = defect_of(2, kept2, forcing2, screening2, 0)[0][0]
    for distance in (1, 2, 4):
        grouped = grouped + lanes_of(grouped, lane ^ distance)

    sums[rank] = grouped[0:1, :] * 0.5
    for k, value in enumerate((kept1, kept2, forcing2)):
        coarse_out[k] = value[0][0]
    arrived = [send(sums.at[rank], sums.at[rank], o, True) for o in range(1, devices)]
    for o in offsets(REACH):
        arrive["coarse", -o] = send(coarse_out, coarse.at[place(-o, REACH)], o)
    kept1, kept2, forcing2 = {0: kept1[0]}, {0: kept2[0]}, {0: forcing2[0]}
    for copy in arrived:
        copy.wait_recv()
    width, base, bases = devices, 0, []
    row = [sums[d] for d in range(devices)]
    while width > 1:
        width //= 2
        row = [row[2 * i] + row[2 * i + 1] for i in range(width)]
        bases.append(base)
        for i in range(width):
            tree[base + i] = row[i]
        base += width

    current = {}
    for j in [0] + offsets(REACH):
        if j:
            arrive["coarse", j].wait_recv()
            for k, field in enumerate((kept1, kept2, forcing2)):
                field[j] = [coarse[place(j, REACH), k]]
        other = at(j)
        correction = sums[other] / COARSE
        for k, base in enumerate(bases, 1):
            correction = correction + tree[base + other // 2**k] / (COARSE * 2**k)
        current[j] = [kept2[j][0] + jnp.where(live[j], jnp.broadcast_to(correction, tile), 0.0)]
    current = sweep(2, current, forcing2, weight2, 3)
    current = sweep(2, current, forcing2, weight2, 2)
    current = {j: [kept1[j][0] + masked(j, v)[0]] for j, v in current.items()}
    current = sweep(1, current, forcing1, weight1, 2)
    current = sweep(1, current, forcing1, weight1, 1)
    for j in (-1, 1):
        arrive["fine", j].wait_recv()
        kept0[j] = [fine[place(j, 1), k] for k in range(8)]
    current = {
        j: [a + jnp.where(live[j], jnp.broadcast_to(v[0][k : k + 1, :], tile), 0.0) for k, a in enumerate(kept0[j])]
        for j, v in current.items()
    }
    current = sweep(0, current, forcing0, weight0, 1)
    current = sweep(0, current, forcing0, weight0, 0)[0]

    spread = (sub & 1) + (sub >> 2) * 2
    upper = (sub & 2) != 0
    for hx in range(2):
        for hy in range(2):
            low, high = current[4 * hx + 2 * hy], current[4 * hx + 2 * hy + 1]
            for bx in range(2):
                row = 8 * (4 * hx + 2 * bx + hy)
                index = spread + 4 * bx
                out[row : row + 8, :] = jnp.where(upper, rows_of(high, index), rows_of(low, index))
    for copy, offset in copies:
        if offset:
            pl.when(reaches(offset))(copy.wait_send)
        else:
            copy.wait_send()


def per_device(rhs, screen, guess, counts, neighbours):
    shape = rhs.shape
    slots = shape[3]
    devices = lax.axis_size("sfc")
    rows = shape[0] * shape[1] * shape[2]
    vmem = pl.BlockSpec(memory_space=pltpu.VMEM)
    result = pl.pallas_call(
        lambda *refs: cycle_kernel(devices, slots, *refs),
        out_shape=jax.ShapeDtypeStruct((rows, slots), jnp.float32),
        in_specs=[pl.BlockSpec(memory_space=pltpu.SMEM)] + [pl.BlockSpec(memory_space=pl.ANY)] * 4,
        out_specs=vmem,
        scratch_shapes=[
            pltpu.VMEM((2, 3, rows, slots), jnp.float32),
            pltpu.VMEM((2, 8, slots), jnp.float32),
            pltpu.VMEM((2 * REACH, *neighbours.shape), jnp.int32),
            pltpu.VMEM((2 * REACH, 2, 8, slots), jnp.float32),
            pltpu.VMEM((2, 8, 8, slots), jnp.float32),
            pltpu.VMEM((2 * REACH, 3, 8, slots), jnp.float32),
            pltpu.VMEM((devices, 1, slots), jnp.float32),
            pltpu.VMEM((devices, 1, slots), jnp.float32),
            pltpu.VMEM((8, slots), jnp.float32),
            pltpu.VMEM((2, 8, slots), jnp.float32),
            pltpu.VMEM((8, 8, slots), jnp.float32),
            pltpu.VMEM((3, 8, slots), jnp.float32),
            pltpu.VMEM((3, rows, slots), jnp.float32),
            pltpu.VMEM(neighbours.shape, jnp.int32),
            pltpu.SemaphoreType.DMA((10 + 6 * REACH + devices - 1,)),
            pltpu.SemaphoreType.DMA((10 + 6 * REACH + devices - 1,)),
            pltpu.SemaphoreType.DMA((4,)),
        ],
        compiler_params=pltpu.CompilerParams(collective_id=0, has_side_effects=True),
        name="cycle",
    )(counts, rhs.reshape(rows, slots), screen.reshape(rows, slots), guess.reshape(rows, slots), neighbours)
    return result.reshape(shape)


def solution(mesh):
    blocks = P(None, None, None, "sfc")
    return jax.shard_map(
        per_device,
        mesh=mesh,
        in_specs=(blocks, blocks, blocks, P(), P(None, "sfc")),
        out_specs=blocks,
        check_vma=False,
    )
```

```python
import jax
import jax.numpy as jnp
from jax import lax
from jax.experimental import pallas as pl
from jax.experimental.pallas import tpu as pltpu
from jax.sharding import PartitionSpec as P

OMEGA = 0.8
COARSE = 8.0
RIM = 8
REACH = 3
MESH = pl.DeviceIdType.MESH


def lanes_of(values, index):
    return jnp.take_along_axis(values, index, axis=1, mode="promise_in_bounds")


def rows_of(values, index):
    return jnp.take_along_axis(values, index, axis=0, mode="promise_in_bounds")


def cycle_kernel(
    devices, slots, counts, rhs_in, screen_in, guess_in, neighbours_in, out,
    near, rim, codes, middle, fine, coarse, sums, tree,
    rim_out, middle_out, fine_out, coarse_out, own, neighbours, send_sem, recv_sem, load_sem,
):
    rank = lax.axis_index("sfc")

    def at(offset):
        return lax.rem(rank + offset + devices, devices)

    guess, rhs, screen = own.at[0], own.at[1], own.at[2]
    pairs = ((guess_in, guess), (rhs_in, rhs), (screen_in, screen), (neighbours_in, neighbours))
    loads = [pltpu.make_async_copy(a, b, load_sem.at[k]) for k, (a, b) in enumerate(pairs)]
    for copy in loads:
        copy.start()

    barrier = pltpu.get_barrier_semaphore()
    for offset in range(1, devices):
        pl.semaphore_signal(barrier, inc=1, device_id=(at(offset),), device_id_type=MESH)

    tile = (8, slots)
    sub = lax.broadcasted_iota(jnp.int32, tile, 0)
    lane = lax.broadcasted_iota(jnp.int32, tile, 1)
    bits = [(sub & (4 >> a)) != 0 for a in range(3)]
    flips = [sub ^ (4 >> a) for a in range(3)]
    half = slots // 2
    live_of = {j: counts[at(j)] for j in range(-REACH - 1, REACH + 1)}
    live = {j: lane < live_of[j] for j in range(-REACH, REACH + 1)}

    pack_place = (lane & (half - 1)) // RIM
    pack_index = {
        j: (lane & (RIM - 1)) + jnp.where(lane < half, live_of[j] - RIM, 0)
        for j in range(-REACH, REACH + 1)
    }

    copies = []

    def reaches(offset):
        return rank < devices - offset if offset > 0 else rank >= -offset

    class Arrival:
        def __init__(self, copy, offset):
            self.copy, self.offset = copy, offset

        def wait_recv(self):
            if self.offset:
                pl.when(reaches(-self.offset))(self.copy.wait_recv)
            else:
                self.copy.wait_recv()

    def send(source, target, offset, wrap=False):
        number = len(copies)
        copy = pltpu.make_async_remote_copy(
            src_ref=source,
            dst_ref=target,
            send_sem=send_sem.at[number],
            recv_sem=recv_sem.at[number],
            device_id=(at(offset),),
            device_id_type=MESH,
        )
        if wrap:
            copy.start()
        else:
            pl.when(reaches(offset))(copy.start)
        copies.append((copy, 0 if wrap else offset))
        return Arrival(copy, 0 if wrap else offset)

    def place(offset, reach):
        return offset + reach if offset < 0 else offset + reach - 1

    def offsets(reach):
        return [sign * step for step in range(1, reach + 1) for sign in (1, -1)]

    first = (sub & 1) + ((sub >> 1) & 1) * 4

    def load(ref, *lead):
        rows = [ref[(*lead, slice(8 * t, 8 * t + 8), slice(None))] for t in range(8)]
        result = []
        for hx in range(2):
            for hy in range(2):
                low, high = rows[4 * hx + hy], rows[4 * hx + 2 + hy]
                for index in (first, first + 2):
                    result.append(jnp.where(sub < 4, rows_of(low, index), rows_of(high, index)))
        return result

    def masked(part, values):
        return [jnp.where(live[part], v, 0.0) for v in values]

    def packed(part, values):
        if len(values) == 1:
            return lanes_of(values[0], pack_index[part])
        result = lanes_of(values[0], pack_index[part])
        for j in range(1, 8):
            result = jnp.where(pack_place == j, lanes_of(values[j], pack_index[part]), result)
        return result

    for copy in loads:
        copy.wait()
    pl.semaphore_wait(barrier, devices - 1)
    arrive = {}
    for o in offsets(1):
        for k, ref in enumerate((guess, rhs, screen)):
            arrive["near", -o, k] = send(ref, near.at[place(-o, 1), k], o)
        arrive["codes", -o] = send(neighbours, codes.at[place(-o, REACH)], o)
    forcing, screening, current = ({0: masked(0, load(r))} for r in (rhs, screen, guess))
    rim_out[...] = packed(0, current[0])
    for o in offsets(2)[2:]:
        arrive["rim", -o] = send(rim_out, rim.at[place(-o, 2) // 3], o)

    def decoded(part, code):
        inside = (code >= slots) & (code < 2 * slots)
        outside = (code >= 0) & jnp.logical_not(inside)
        local = jnp.where(inside, code - slots, 0)
        off = jnp.where(code < slots, code - (live_of[part - 1] - RIM), half + code - 2 * slots)
        return inside, outside, local, jnp.where(outside, off & (slots - 1), 0)

    tables = {}

    def table(part):
        if part not in tables:
            if part:
                arrive["codes", part].wait_recv()
                ref = codes.at[place(part, REACH)]
            else:
                ref = neighbours
            rows = [jnp.broadcast_to(ref[k : k + 1, :], tile) for k in range(6)]
            sided = [decoded(part, jnp.where(bits[a], rows[2 * a], rows[2 * a + 1])) for a in range(3)]
            taker = [decoded(part, jnp.where(bits[a], rows[2 * a + 1], rows[2 * a])) for a in range(3)]
            every = jnp.full(tile, -1, jnp.int32)
            for k in range(6):
                every = jnp.where(sub == k, rows[k], every)
            tables[part] = (sided, taker, decoded(part, every))
        return tables[part]

    def total_fine(part, values, received):
        sided, taker, _ = table(part)
        total = [None] * 8
        for a in range(3):
            stride = 4 >> a
            inside, _, local, _ = sided[a]
            _, outside, _, off = taker[a]
            turned = rows_of(received, flips[a])
            base = off + jnp.where(bits[a], 0, RIM * stride)
            for j in range(8):
                if j & stride:
                    continue
                low, high = values[j], values[j + stride]
                across = jnp.where(inside, lanes_of(jnp.where(bits[a], high, low), local), 0.0)
                got = jnp.where(outside, lanes_of(turned, (base + RIM * j) & (slots - 1)), 0.0)
                for where, kept, far in (
                    (j, low + jnp.where(bits[a], across, high), jnp.where(bits[a], 0.0, got)),
                    (j + stride, high + jnp.where(bits[a], low, across), jnp.where(bits[a], got, 0.0)),
                ):
                    piece = rows_of(kept, flips[a]) + far
                    total[where] = piece if total[where] is None else total[where] + piece
        return total

    def total_middle(part, values, received):
        sided, taker, _ = table(part)
        total = None
        for a in range(3):
            inside, _, local, _ = sided[a]
            _, outside, _, off = taker[a]
            piece = rows_of(values[0] + jnp.where(inside, lanes_of(values[0], local), 0.0), flips[a])
            piece = piece + jnp.where(outside, lanes_of(rows_of(received, flips[a]), off), 0.0)
            total = piece if total is None else total + piece
        return [total]

    def total_coarse(part, values, received):
        inside, outside, local, off = table(part)[2]
        piece = jnp.where(inside, lanes_of(values[0], local), 0.0)
        piece = piece + jnp.where(outside, lanes_of(received, off), 0.0)
        return [jnp.broadcast_to(piece.sum(axis=0, keepdims=True), tile)]

    totals = (total_fine, total_middle, total_coarse)

    def total(depth, values, reach, rims=None, parts=None):
        rims = dict(rims or {})
        for j in values:
            if abs(j) <= reach + 1:
                rims[j] = packed(j, values[j])
        result = {}
        for j in parts or range(-reach, reach + 1):
            lower, upper = rims.get(j - 1), rims.get(j + 1)
            received = upper if lower is None else lower if upper is None else jnp.where(lane < half, lower, upper)
            result[j] = totals[depth](j, values[j], received)
        return result

    def sweep(depth, values, forcing, weight, reach, rims=None, parts=None):
        found = total(depth, values, reach, rims, parts)
        return {
            j: [(1.0 - OMEGA) * v + w * (f + t) for v, f, w, t in zip(values[j], forcing[j], weight[j], found[j])]
            for j in found
        }

    def defect_of(depth, values, forcing, screening, reach):
        found = total(depth, values, reach)
        return {
            j: masked(j, [f - ((6.0 + s) * v - t) for v, f, s, t in zip(values[j], forcing[j], screening[j], found[j])])
            for j in found
        }

    def weights(screening):
        return {j: masked(j, [OMEGA / (6.0 + s) for s in values]) for j, values in screening.items()}

    def start(forcing, weight):
        return {j: [w * f for w, f in zip(weight[j], forcing[j])] for j in forcing}

    def restrict_fine(values):
        result = jnp.broadcast_to(values[0].sum(axis=0, keepdims=True), tile)
        for j in range(1, 8):
            result = jnp.where(sub == j, values[j].sum(axis=0, keepdims=True), result)
        return [result * 0.5]

    def restrict_middle(values):
        return [jnp.broadcast_to(values[0].sum(axis=0, keepdims=True) * 0.5, tile)]

    own_weight = weights(screening)
    for j in (-1, 1):
        arrive["near", j, 0].wait_recv()
        current[j] = masked(j, load(near, place(j, 1), 0))
    swept = sweep(0, current, forcing, own_weight, 0)
    for o in offsets(REACH)[2:]:
        arrive["codes", -o] = send(neighbours, codes.at[place(-o, REACH)], o)
    for j in (-1, 1):
        for k, field in ((1, forcing), (2, screening)):
            arrive["near", j, k].wait_recv()
            field[j] = masked(j, load(near, place(j, 1), k))
    weight0, forcing0 = weights(screening), forcing
    rims = {}
    for j in (-2, 2):
        arrive["rim", j].wait_recv()
        rims[j] = rim[place(j, 2) // 3]
    current = {**swept, **sweep(0, current, forcing, weight0, 1, rims, (-1, 1))}
    kept0 = sweep(0, current, forcing, weight0, 1)
    for j in range(8):
        fine_out[j] = kept0[0][j]
    defect = defect_of(0, kept0, forcing, screening, 0)
    kept0 = {0: kept0[0]}
    forcing1, screening1 = {0: restrict_fine(defect[0])}, {0: restrict_fine(screening[0])}

    middle_out[0] = forcing1[0][0]
    middle_out[1] = screening1[0][0]
    for o in offsets(REACH):
        arrive["middle", -o] = send(middle_out, middle.at[place(-o, REACH)], o)
    for o in offsets(1):
        arrive["fine", -o] = send(fine_out, fine.at[place(-o, 1)], o)
    for j in offsets(REACH):
        table(j)
        arrive["middle", j].wait_recv()
        forcing1[j] = [middle[place(j, REACH), 0]]
        screening1[j] = [middle[place(j, REACH), 1]]
    weight1 = weights(screening1)
    kept1 = sweep(1, start(forcing1, weight1), forcing1, weight1, 2)
    forcing2 = {j: restrict_middle(v) for j, v in defect_of(1, kept1, forcing1, screening1, 1).items()}
    screening2 = {j: restrict_middle(v) for j, v in screening1.items()}
    weight2 = weights(screening2)
    kept2 = sweep(2, start(forcing2, weight2), forcing2, weight2, 1)
    grouped = defect_of(2, kept2, forcing2, screening2, 0)[0][0]
    for distance in (1, 2, 4):
        grouped = grouped + lanes_of(grouped, lane ^ distance)

    sums[rank] = grouped[0:1, :] * 0.5
    for k, value in enumerate((kept1, kept2, forcing2)):
        coarse_out[k] = value[0][0]
    arrived = [send(sums.at[rank], sums.at[rank], o, True) for o in range(1, devices)]
    for o in offsets(REACH):
        arrive["coarse", -o] = send(coarse_out, coarse.at[place(-o, REACH)], o)
    kept1, kept2, forcing2 = {0: kept1[0]}, {0: kept2[0]}, {0: forcing2[0]}
    for copy in arrived:
        copy.wait_recv()
    width, base, bases = devices, 0, []
    row = [sums[d] for d in range(devices)]
    while width > 1:
        width //= 2
        row = [row[2 * i] + row[2 * i + 1] for i in range(width)]
        bases.append(base)
        for i in range(width):
            tree[base + i] = row[i]
        base += width

    current = {}
    for j in [0] + offsets(REACH):
        if j:
            arrive["coarse", j].wait_recv()
            for k, field in enumerate((kept1, kept2, forcing2)):
                field[j] = [coarse[place(j, REACH), k]]
        other = at(j)
        correction = sums[other] / COARSE
        for k, base in enumerate(bases, 1):
            correction = correction + tree[base + other // 2**k] / (COARSE * 2**k)
        current[j] = [kept2[j][0] + jnp.where(live[j], jnp.broadcast_to(correction, tile), 0.0)]
    current = sweep(2, current, forcing2, weight2, 3)
    current = sweep(2, current, forcing2, weight2, 2)
    current = {j: [kept1[j][0] + masked(j, v)[0]] for j, v in current.items()}
    current = sweep(1, current, forcing1, weight1, 2)
    current = sweep(1, current, forcing1, weight1, 1)
    for j in (-1, 1):
        arrive["fine", j].wait_recv()
        kept0[j] = [fine[place(j, 1), k] for k in range(8)]
    current = {
        j: [a + jnp.where(live[j], jnp.broadcast_to(v[0][k : k + 1, :], tile), 0.0) for k, a in enumerate(kept0[j])]
        for j, v in current.items()
    }
    current = sweep(0, current, forcing0, weight0, 1)
    current = sweep(0, current, forcing0, weight0, 0)[0]

    spread = (sub & 1) + (sub >> 2) * 2
    upper = (sub & 2) != 0
    for hx in range(2):
        for hy in range(2):
            low, high = current[4 * hx + 2 * hy], current[4 * hx + 2 * hy + 1]
            for bx in range(2):
                row = 8 * (4 * hx + 2 * bx + hy)
                index = spread + 4 * bx
                out[row : row + 8, :] = jnp.where(upper, rows_of(high, index), rows_of(low, index))
    for copy, offset in copies:
        if offset:
            pl.when(reaches(offset))(copy.wait_send)
        else:
            copy.wait_send()


def per_device(rhs, screen, guess, counts, neighbours):
    shape = rhs.shape
    slots = shape[3]
    devices = lax.axis_size("sfc")
    rows = shape[0] * shape[1] * shape[2]
    vmem = pl.BlockSpec(memory_space=pltpu.VMEM)
    result = pl.pallas_call(
        lambda *refs: cycle_kernel(devices, slots, *refs),
        out_shape=jax.ShapeDtypeStruct((rows, slots), jnp.float32),
        in_specs=[pl.BlockSpec(memory_space=pltpu.SMEM)] + [pl.BlockSpec(memory_space=pl.ANY)] * 4,
        out_specs=vmem,
        scratch_shapes=[
            pltpu.VMEM((2, 3, rows, slots), jnp.float32),
            pltpu.VMEM((2, 8, slots), jnp.float32),
            pltpu.VMEM((2 * REACH, *neighbours.shape), jnp.int32),
            pltpu.VMEM((2 * REACH, 2, 8, slots), jnp.float32),
            pltpu.VMEM((2, 8, 8, slots), jnp.float32),
            pltpu.VMEM((2 * REACH, 3, 8, slots), jnp.float32),
            pltpu.VMEM((devices, 1, slots), jnp.float32),
            pltpu.VMEM((devices, 1, slots), jnp.float32),
            pltpu.VMEM((8, slots), jnp.float32),
            pltpu.VMEM((2, 8, slots), jnp.float32),
            pltpu.VMEM((8, 8, slots), jnp.float32),
            pltpu.VMEM((3, 8, slots), jnp.float32),
            pltpu.VMEM((3, rows, slots), jnp.float32),
            pltpu.VMEM(neighbours.shape, jnp.int32),
            pltpu.SemaphoreType.DMA((10 + 6 * REACH + devices - 1,)),
            pltpu.SemaphoreType.DMA((10 + 6 * REACH + devices - 1,)),
            pltpu.SemaphoreType.DMA((4,)),
        ],
        compiler_params=pltpu.CompilerParams(collective_id=0, has_side_effects=True),
        name="cycle",
    )(counts, rhs.reshape(rows, slots), screen.reshape(rows, slots), guess.reshape(rows, slots), neighbours)
    return result.reshape(shape)


def solution(mesh):
    blocks = P(None, None, None, "sfc")
    return jax.shard_map(
        per_device,
        mesh=mesh,
        in_specs=(blocks, blocks, blocks, P(), P(None, "sfc")),
        out_specs=blocks,
        check_vma=False,
    )
```
